128 devices in a mesh: lon: 16 (over x, y), lat: 8 (over z, core).
Axes of the slice: x: 4, y: 4, z: 4, core: 2. Of those that a mesh axis runs over, the one named last changes fastest.
Arguments:
- fields: float32 [4, 64, 1024, 128], P(None, 'lon', 'lat'), may hold values from -6 to 6
- mixing: float32 [4, 4, 128, 128], replicated
- classes: int32 [64, 1024], P('lon', 'lat'), may hold values from 0 to 15
Outputs:
- smoothed: float32 [4, 64, 1024, 128], P(None, 'lon', 'lat')
The draws below stay inside these ranges and needn't reach their ends.
All inputs are finite; a program needn't handle non-finite values.
Results may differ from the reference program's by a relative error of at most 0.0003.
Values sent between devices are 32-bit elements; how exact they have to be, the bound alone decides.
A program may use at most 64 MiB of HBM per device.

```python
import math
import jax
import jax.numpy as jnp
from jax import lax

NF = 4
LEV = 128
OPS = 4
STEPS = 16
NLON = 64
NLAT = 1024


def draw_mixing(key, part):
    key = jax.random.fold_in(key, 11)
    diagonal_key, spread_key = jax.random.split(key)
    scatter = jax.random.normal(spread_key, (NF, OPS, LEV, LEV), jnp.float32) * (0.2 / math.sqrt(LEV))
    diagonal = jax.random.uniform(diagonal_key, (NF, OPS, LEV), jnp.float32, 0.8, 1.0)
    identity = jnp.eye(LEV, dtype=jnp.float32)
    return scatter * (1.0 - identity) + identity * diagonal[:, :, :, None]


def draw_classes(key, part):
    key = jax.random.fold_in(key, 23)
    band_key, heavy_key, light_key = jax.random.split(key, 3)
    band_rows = NLAT // 4
    band_start = jax.random.randint(band_key, (), 0, NLAT - band_rows + 1, dtype=jnp.int32)
    latitude = jnp.arange(NLAT, dtype=jnp.int32)[None, :]
    inside = (latitude >= band_start) & (latitude < band_start + band_rows)
    heavy_class = jax.random.randint(heavy_key, (NLON, NLAT), STEPS // 2, STEPS, dtype=jnp.int32)
    light_class = jax.random.randint(light_key, (NLON, NLAT), 0, STEPS // 4, dtype=jnp.int32)
    return jnp.where(inside, heavy_class, light_class).astype(jnp.int32)


def level_of(key, shape, cuts, low, largest):
    level, own = 1.0, jax.random.fold_in(key, 6)
    for dim, parts in cuts:
        draws = jnp.exp(jax.random.uniform(jax.random.fold_in(own, dim), (parts,), jnp.float32, low / len(cuts), largest / len(cuts)))
        level = level * jnp.repeat(draws, shape[dim] // parts).reshape([-1 if axis == dim else 1 for axis in range(len(shape))])
    return level


def normal_values(rng, extent, spread, bound, cuts=(), kind=jnp.bfloat16):
    gain = level_of(rng, extent, cuts, -0.22, 0.18) if cuts else 1.0
    result = jax.random.normal(rng, extent, jnp.float32) * spread * gain
    return jnp.minimum(jnp.maximum(result, -bound), bound).astype(kind)


def setup_inputs(seed: int = 0) -> dict:
    arg_keys = jax.random.split(jax.random.key(seed), 4)
    fields = normal_values(arg_keys[0], (NF, NLON, NLAT, LEV), 1.0, 6.0, ((1, 16), (2, 8)), jnp.float32)
    mixing = draw_mixing(jax.random.fold_in(arg_keys[3], 71), 0)
    classes = draw_classes(jax.random.fold_in(arg_keys[3], 71), 0)
    return dict(fields=fields, mixing=mixing, classes=classes)


smoothing_rate = 0.2
limit_scale = 2.0


def chain(values, mixing):
    for operator_index in range(OPS):
        mixed = jnp.einsum('fcb,fab->fca', values, mixing[:, operator_index], precision=lax.Precision.HIGHEST)
        values = limit_scale * jnp.tanh(mixed / limit_scale)
    return values


def reference(fields, mixing, classes):
    total = NLON * NLAT
    flat = fields.reshape(NF, total, LEV)
    substeps = (classes + 1).reshape(total).astype(jnp.int32)
    ordering = jnp.argsort(substeps, stable=True)
    inverse = jnp.argsort(ordering, stable=True)
    ordered = jnp.take(flat, ordering, axis=1)
    ordered_steps = jnp.take(substeps, ordering, axis=0).astype(jnp.int32)
    block_cols = 4096 if total % 4096 == 0 else total
    block_count = total // block_cols
    blocks = jnp.transpose(ordered.reshape(NF, block_count, block_cols, LEV), (1, 0, 2, 3))
    block_steps = ordered_steps.reshape(block_count, block_cols)

    def one_block(pair):
        data, counts = pair

        def substep(turn_index, current):
            updated = chain(current, mixing)
            return jnp.where((turn_index < counts)[None, :, None], updated, current)

        return lax.fori_loop(jnp.int32(0), jnp.max(counts).astype(jnp.int32), substep, data)

    advanced = lax.map(one_block, (blocks, block_steps))
    ordered_done = jnp.transpose(advanced, (1, 0, 2, 3)).reshape(NF, total, LEV)
    column_state = jnp.take(ordered_done, inverse, axis=1).reshape(NF, NLON, NLAT, LEV)
    eastern = jnp.roll(column_state, -1, axis=1)
    western = jnp.roll(column_state, 1, axis=1)
    northern = jnp.concatenate([column_state[:, :, 1:], column_state[:, :, -1:]], axis=2)
    southern = jnp.concatenate([column_state[:, :, :1], column_state[:, :, :-1]], axis=2)
    return column_state + smoothing_rate * (eastern + western + northern + southern - 4.0 * column_state)
```

```python
import functools

import jax
import jax.numpy as jnp
from jax import lax
from jax.experimental import pallas as pl
from jax.experimental.pallas import tpu as pltpu
from jax.sharding import PartitionSpec as P

STEPS = 16
UNROLL = 4
PAD = 16
MESH = pl.DeviceIdType.MESH


def split(values):
    high = values.astype(jnp.bfloat16)
    low = (values - high.astype(jnp.float32)).astype(jnp.bfloat16)
    return high, low


def advance(state, limits, weights):
    field_count, ops = weights.shape[0], weights.shape[1]

    def substeps(turn, _):
        current = [state[f] for f in range(field_count)]
        for k in range(UNROLL):
            active = limits[...] > turn * UNROLL + k
            values = list(current)
            for o in range(ops):
                for f in range(field_count):
                    pieces = jnp.concatenate(split(values[f]), axis=1)
                    mixed = jnp.dot(pieces, weights[f, o], preferred_element_type=jnp.float32)
                    half = mixed.shape[1] // 2
                    values[f] = jnp.tanh(mixed[:, :half] + mixed[:, half:])
            current = [jnp.where(active, new, old) for new, old in zip(values, current)]
        for f in range(field_count):
            state[f] = current[f]
        return 0

    lax.fori_loop(0, STEPS // UNROLL, substeps, 0)


def kernel(
    fields, mixing, classes, out,
    outer, inner, outer_limits, inner_limits, matrices, weights,
    north_send, south_send, east_halo, west_halo, north_halo, south_halo, result,
    load_sem, mix_sem, send_sem, recv_sem, out_sem,
):
    field_count, lons, lats, levels = fields.shape
    ops = mixing.shape[1]
    lon, lat = lax.axis_index("lon"), lax.axis_index("lat")
    lon_count, lat_count = lax.axis_size("lon"), lax.axis_size("lat")
    east = (lax.rem(lon + 1, lon_count), lat)
    west = (lax.rem(lon + lon_count - 1, lon_count), lat)
    north = (lon, lax.rem(lat + 1, lat_count))
    south = (lon, lax.rem(lat + lat_count - 1, lat_count))

    mix_copy = pltpu.make_async_copy(mixing, matrices, mix_sem)
    mix_copy.start()
    places = [(outer, 0), (inner, 0), (inner, lats), (outer, lats)]
    loads = []
    for f in range(field_count):
        for i in range(lons):
            buffer, row = places[i]
            copy = pltpu.make_async_copy(
                fields.at[f, i], buffer.at[f, pl.ds(row, lats)], load_sem.at[f * lons + i]
            )
            copy.start()
            loads.append(copy)

    barrier = pltpu.get_barrier_semaphore()
    for neighbour in (east, west, north, south):
        pl.semaphore_signal(barrier, inc=1, device_id=neighbour, device_id_type=MESH)

    edge_rows = []
    for i in range(lons):
        buffer, row = (outer_limits, places[i][1]) if i in (0, lons - 1) else (inner_limits, places[i][1])
        limit = jnp.broadcast_to(classes[pl.ds(i, 1), :] + 1, (levels, lats)).T
        buffer[pl.ds(row, lats), :] = limit
        if i in (1, 2):
            edge_rows += [limit[:1], limit[lats - 1:]]
    outer_limits[pl.ds(2 * lats, PAD), :] = jnp.concatenate(
        edge_rows + [jnp.zeros((PAD - 4, levels), jnp.int32)], axis=0
    )

    mix_copy.wait()
    for f in range(field_count):
        for o in range(ops):
            pieces = jnp.concatenate(split(matrices[f, o]), axis=0).T
            weights[f, o, pl.ds(0, levels), :] = pieces
            weights[f, o, pl.ds(levels, levels), :] = pieces

    for copy in loads:
        copy.wait()
    for f in range(field_count):
        outer[f, pl.ds(0, 2 * lats), :] = 0.5 * outer[f, pl.ds(0, 2 * lats), :]
        inner[f] = 0.5 * inner[f]
        outer[f, pl.ds(2 * lats, PAD), :] = jnp.concatenate(
            [
                inner[f, pl.ds(0, 1), :],
                inner[f, pl.ds(lats - 1, 1), :],
                inner[f, pl.ds(lats, 1), :],
                inner[f, pl.ds(2 * lats - 1, 1), :],
                jnp.zeros((PAD - 4, levels), jnp.float32),
            ],
            axis=0,
        )

    advance(outer, outer_limits, weights)

    low_rows = (0, 2 * lats, 2 * lats + 2, lats)
    high_rows = (lats - 1, 2 * lats + 1, 2 * lats + 3, 2 * lats - 1)
    for f in range(field_count):
        for i in range(lons):
            south_send[pl.ds(f * lons + i, 1), :] = outer[f, pl.ds(low_rows[i], 1), :]
            north_send[pl.ds(f * lons + i, 1), :] = outer[f, pl.ds(high_rows[i], 1), :]

    pl.semaphore_wait(barrier, 4)
    copies = []

    def send(source, target, device):
        slot = len(copies)
        copy = pltpu.make_async_remote_copy(
            src_ref=source, dst_ref=target, send_sem=send_sem.at[slot], recv_sem=recv_sem.at[slot],
            device_id=device, device_id_type=MESH,
        )
        copy.start()
        copies.append(copy)

    send(north_send, south_halo, north)
    send(south_send, north_halo, south)
    for f in range(field_count):
        send(outer.at[f, pl.ds(lats, lats)], west_halo.at[f], east)
        send(outer.at[f, pl.ds(0, lats)], east_halo.at[f], west)

    advance(inner, inner_limits, weights)

    for copy in copies:
        copy.wait()

    row = lax.broadcasted_iota(jnp.int32, (lats, levels), 0)
    stores = []
    for f in range(field_count):
        cells = [
            outer[f, pl.ds(0, lats), :],
            inner[f, pl.ds(0, lats), :],
            inner[f, pl.ds(lats, lats), :],
            outer[f, pl.ds(lats, lats), :],
        ]
        around = [west_halo[f]] + cells + [east_halo[f]]
        for i in range(lons):
            cell = cells[i]
            k = f * lons + i
            above = jnp.where(lat == lat_count - 1, cell[lats - 1:], north_halo[pl.ds(k, 1), :])
            below = jnp.where(lat == 0, cell[:1], south_halo[pl.ds(k, 1), :])
            northern = jnp.where(row == lats - 1, above, pltpu.roll(cell, lats - 1, 0))
            southern = jnp.where(row == 0, below, pltpu.roll(cell, 1, 0))
            result[f, i] = 0.4 * (cell + around[i] + around[i + 2] + northern + southern)
        copy = pltpu.make_async_copy(result.at[f], out.at[f], out_sem.at[f])
        copy.start()
        stores.append(copy)
    for copy in stores:
        copy.wait()


def per_device(fields, mixing, classes):
    field_count, lons, lats, levels = fields.shape
    ops = mixing.shape[1]
    f32, i32 = jnp.float32, jnp.int32
    halo = pltpu.VMEM((field_count, lats, levels), f32)
    edge = pltpu.VMEM((field_count * lons, levels), f32)
    copies = 2 + 2 * field_count
    rows = STEPS * ops * field_count * (lons * lats + PAD)
    return pl.pallas_call(
        kernel,
        out_shape=jax.ShapeDtypeStruct(fields.shape, f32),
        in_specs=[
            pl.BlockSpec(memory_space=pl.ANY),
            pl.BlockSpec(memory_space=pl.ANY),
            pl.BlockSpec(memory_space=pltpu.VMEM),
        ],
        out_specs=pl.BlockSpec(memory_space=pl.ANY),
        scratch_shapes=[
            pltpu.VMEM((field_count, 2 * lats + PAD, levels), f32),
            pltpu.VMEM((field_count, 2 * lats, levels), f32),
            pltpu.VMEM((2 * lats + PAD, levels), i32),
            pltpu.VMEM((2 * lats, levels), i32),
            pltpu.VMEM(mixing.shape, f32),
            pltpu.VMEM((field_count, ops, 2 * levels, 2 * levels), jnp.bfloat16),
            edge, edge, halo, halo, edge, edge,
            pltpu.VMEM(fields.shape, f32),
            pltpu.SemaphoreType.DMA((field_count * lons,)),
            pltpu.SemaphoreType.DMA,
            pltpu.SemaphoreType.DMA((copies,)),
            pltpu.SemaphoreType.DMA((copies,)),
            pltpu.SemaphoreType.DMA((field_count,)),
        ],
        compiler_params=pltpu.CompilerParams(
            collective_id=0, has_side_effects=True, vmem_limit_bytes=40 * 2**20
        ),
        cost_estimate=pl.CostEstimate(
            flops=2 * rows * (2 * levels) ** 2, bytes_accessed=12 * 2**20 // 4, transcendentals=rows * levels
        ),
    )(fields, mixing, classes)


def solution(mesh):
    in_specs = (P(None, "lon", "lat", None), P(), P("lon", "lat"))
    out_specs = P(None, "lon", "lat", None)
    return jax.shard_map(
        per_device, mesh=mesh, in_specs=in_specs, out_specs=out_specs, check_vma=False
    )
```

```python
import functools

import jax
import jax.numpy as jnp
from jax import lax
from jax.experimental import pallas as pl
from jax.experimental.pallas import tpu as pltpu
from jax.sharding import PartitionSpec as P

STEPS = 16
HEAD = 4
PAD = 16
MESH = pl.DeviceIdType.MESH


def split(values):
    high = values.astype(jnp.bfloat16)
    low = (values - high.astype(jnp.float32)).astype(jnp.bfloat16)
    return high, low


def advance(units, count, weights):
    current = [state[f] for state, _, f, _ in units]
    for _ in range(count):
        values = list(current)
        for o in range(weights.shape[1]):
            for k, (_, _, f, _) in enumerate(units):
                pieces = jnp.concatenate(split(values[k]), axis=1)
                mixed = jnp.dot(pieces, weights[f, o], preferred_element_type=jnp.float32)
                half = mixed.shape[1] // 2
                values[k] = jnp.tanh(mixed[:, :half] + mixed[:, half:])
        for k, unit in enumerate(units):
            current[k] = jnp.where(unit[1][...] > unit[3], values[k], current[k])
            unit[3] += 1
    for k, (state, _, f, _) in enumerate(units):
        state[f] = current[k]


def kernel(
    fields, mixing, classes,
    outer, inner, east_halo, west_halo, north_halo, south_halo,
    outer_limits, inner_limits, matrices, weights, steps, north_send, south_send,
    load_sem, mix_sem, class_sem, send_sem, recv_sem,
):
    field_count, lons, lats, levels = fields.shape
    ops = mixing.shape[1]
    lon, lat = lax.axis_index("lon"), lax.axis_index("lat")
    lon_count, lat_count = lax.axis_size("lon"), lax.axis_size("lat")
    east = (lax.rem(lon + 1, lon_count), lat)
    west = (lax.rem(lon + lon_count - 1, lon_count), lat)
    north = (lon, lax.rem(lat + 1, lat_count))
    south = (lon, lax.rem(lat + lat_count - 1, lat_count))
    places = [(outer, 0), (inner, 0), (inner, lats), (outer, lats)]

    def load(chosen):
        copies = []
        for f in chosen:
            copies.append(pltpu.make_async_copy(mixing.at[f], matrices.at[f], mix_sem.at[f]))
            for i in (0, lons - 1, 1, 2):
                buffer, row = places[i]
                copies.append(pltpu.make_async_copy(
                    fields.at[f, i], buffer.at[f, pl.ds(row, lats)], load_sem.at[f * lons + i]
                ))
        for copy in copies:
            copy.start()
        return copies

    def prepare(chosen):
        for f in chosen:
            for o in range(ops):
                pieces = jnp.concatenate(split(matrices[f, o]), axis=0).T
                weights[f, o, pl.ds(0, levels), :] = pieces
                weights[f, o, pl.ds(levels, levels), :] = pieces
            outer[f, pl.ds(0, 2 * lats), :] = 0.5 * outer[f, pl.ds(0, 2 * lats), :]
            inner[f] = 0.5 * inner[f]
            outer[f, pl.ds(2 * lats, PAD), :] = jnp.concatenate(
                [inner[f, pl.ds(r, 1), :] for r in (0, lats - 1, lats, 2 * lats - 1)]
                + [jnp.zeros((PAD - 4, levels), jnp.float32)],
                axis=0,
            )

    class_copy = pltpu.make_async_copy(classes, steps, class_sem)
    class_copy.start()
    first, second = range(field_count // 2), range(field_count // 2, field_count)
    loads = load(first)

    barrier = pltpu.get_barrier_semaphore()
    for neighbour in (east, west, north, south):
        pl.semaphore_signal(barrier, inc=1, device_id=neighbour, device_id_type=MESH)

    class_copy.wait()
    edge_rows = []
    for i in range(lons):
        buffer, row = (outer_limits, places[i][1]) if i in (0, lons - 1) else (inner_limits, places[i][1])
        limit = jnp.broadcast_to(steps[pl.ds(i, 1), :] + 1, (levels, lats)).T
        buffer[pl.ds(row, lats), :] = limit
        if i in (1, 2):
            edge_rows += [limit[:1], limit[lats - 1:]]
    outer_limits[pl.ds(2 * lats, PAD), :] = jnp.concatenate(
        edge_rows + [jnp.zeros((PAD - 4, levels), jnp.int32)], axis=0
    )

    outers = [[outer, outer_limits, f, 0] for f in range(field_count)]
    inners = [[inner, inner_limits, f, 0] for f in range(field_count)]
    for copy in loads:
        copy.wait()
    loads = load(second)
    prepare(first)
    advance([outers[f] for f in first] + [inners[f] for f in first], HEAD, weights)
    for copy in loads:
        copy.wait()
    prepare(second)
    advance(outers, STEPS - HEAD, weights)

    pl.semaphore_wait(barrier, 4)
    copies = []

    def send(source, target, device):
        slot = len(copies)
        copy = pltpu.make_async_remote_copy(
            src_ref=source, dst_ref=target, send_sem=send_sem.at[slot], recv_sem=recv_sem.at[slot],
            device_id=device, device_id_type=MESH,
        )
        copy.start()
        copies.append(copy)

    def send_outer(chosen):
        for f in chosen:
            send(outer.at[f, pl.ds(lats, lats)], west_halo.at[f], east)
            send(outer.at[f, pl.ds(0, lats)], east_halo.at[f], west)

    send_outer(first)
    advance([outers[f] for f in second] + [inners[f] for f in second], HEAD, weights)
    send_outer(second)
    low_rows = (0, 2 * lats, 2 * lats + 2, lats)
    high_rows = (lats - 1, 2 * lats + 1, 2 * lats + 3, 2 * lats - 1)
    for f in range(field_count):
        for i in range(lons):
            south_send[pl.ds(f * lons + i, 1), :] = outer[f, pl.ds(low_rows[i], 1), :]
            north_send[pl.ds(f * lons + i, 1), :] = outer[f, pl.ds(high_rows[i], 1), :]
    send(north_send, south_halo, north)
    send(south_send, north_halo, south)

    advance(inners, STEPS - HEAD, weights)

    for copy in copies:
        copy.wait()


def smooth(outer, inner, east_halo, west_halo, north_halo, south_halo, out, result, out_sem):
    field_count, lons, lats, levels = out.shape
    lat, lat_count = lax.axis_index("lat"), lax.axis_size("lat")
    row = lax.broadcasted_iota(jnp.int32, (lats, levels), 0)
    stores = []
    for f in range(field_count):
        cells = [
            outer[f, pl.ds(0, lats), :],
            inner[f, pl.ds(0, lats), :],
            inner[f, pl.ds(lats, lats), :],
            outer[f, pl.ds(lats, lats), :],
        ]
        around = [west_halo[f]] + cells + [east_halo[f]]
        for i in range(lons):
            cell = cells[i]
            k = f * lons + i
            above = jnp.where(lat == lat_count - 1, cell[lats - 1:], north_halo[pl.ds(k, 1), :])
            below = jnp.where(lat == 0, cell[:1], south_halo[pl.ds(k, 1), :])
            northern = jnp.where(row == lats - 1, above, pltpu.roll(cell, lats - 1, 0))
            southern = jnp.where(row == 0, below, pltpu.roll(cell, 1, 0))
            result[f, i] = 0.4 * (cell + around[i] + around[i + 2] + northern + southern)
            copy = pltpu.make_async_copy(result.at[f, i], out.at[f, i], out_sem.at[k])
            copy.start()
            stores.append(copy)
    for copy in stores:
        copy.wait()


def per_device(fields, mixing, classes):
    field_count, lons, lats, levels = fields.shape
    ops = mixing.shape[1]
    f32, i32 = jnp.float32, jnp.int32
    halo = pltpu.VMEM((field_count, lats, levels), f32)
    edge = pltpu.VMEM((field_count * lons, levels), f32)
    copies = 2 + 2 * field_count
    rows = STEPS * ops * field_count * (lons * lats + PAD)
    in_hbm = pl.BlockSpec(memory_space=pltpu.HBM)
    in_vmem = pl.BlockSpec(memory_space=pltpu.VMEM)
    state = pl.pallas_call(
        kernel,
        out_shape=[
            pltpu.VMEM((field_count, 2 * lats + PAD, levels), f32),
            pltpu.VMEM((field_count, 2 * lats, levels), f32),
            halo, halo, edge, edge,
        ],
        in_specs=[in_hbm] * 3,
        out_specs=[in_vmem] * 6,
        scratch_shapes=[
            pltpu.VMEM((2 * lats + PAD, levels), i32),
            pltpu.VMEM((2 * lats, levels), i32),
            pltpu.VMEM(mixing.shape, f32),
            pltpu.VMEM((field_count, ops, 2 * levels, 2 * levels), jnp.bfloat16),
            pltpu.VMEM((lons, lats), i32),
            edge, edge,
            pltpu.SemaphoreType.DMA((field_count * lons,)),
            pltpu.SemaphoreType.DMA((field_count,)),
            pltpu.SemaphoreType.DMA,
            pltpu.SemaphoreType.DMA((copies,)),
            pltpu.SemaphoreType.DMA((copies,)),
        ],
        compiler_params=pltpu.CompilerParams(
            collective_id=0, has_side_effects=True, vmem_limit_bytes=32 * 2**20
        ),
        cost_estimate=pl.CostEstimate(
            flops=2 * rows * (2 * levels) ** 2, bytes_accessed=2 * 4 * fields.size, transcendentals=rows * levels
        ),
    )(*[pltpu.with_memory_space_constraint(x, pltpu.HBM) for x in (fields, mixing, classes)])
    return pl.pallas_call(
        smooth,
        out_shape=pltpu.HBM(fields.shape, f32),
        in_specs=[in_vmem] * 6,
        out_specs=in_hbm,
        scratch_shapes=[
            pltpu.VMEM(fields.shape, f32),
            pltpu.SemaphoreType.DMA((field_count * lons,)),
        ],
        compiler_params=pltpu.CompilerParams(vmem_limit_bytes=16 * 2**20),
        cost_estimate=pl.CostEstimate(flops=7 * fields.size, bytes_accessed=12 * fields.size, transcendentals=0),
    )(*state)


def solution(mesh):
    in_specs = (P(None, "lon", "lat", None), P(), P("lon", "lat"))
    out_specs = P(None, "lon", "lat", None)
    return jax.shard_map(
        per_device, mesh=mesh, in_specs=in_specs, out_specs=out_specs, check_vma=False
    )
```

```python
import functools

import jax
import jax.numpy as jnp
from jax import lax
from jax.experimental import pallas as pl
from jax.experimental.pallas import tpu as pltpu
from jax.sharding import PartitionSpec as P

STEPS = 16
PAD = 16
MESH = pl.DeviceIdType.MESH


def stretches(field_count):
    left = {(i, f): STEPS for f in range(field_count) for i in (3, 0, 1, 2)}

    def stretch(count, always, shares, fill):
        shares, rounds = dict(shares), []
        for _ in range(count):
            units = [unit for unit in always if left[unit]]
            some = sorted((unit for unit in shares if shares[unit]), key=lambda unit: -shares[unit])
            units += some[:max(0, fill - len(units))]
            for unit in units:
                if unit in shares:
                    shares[unit] -= 1
            inner = sorted(
                (unit for unit in left if unit[0] in (1, 2) and left[unit] and unit not in units),
                key=lambda unit: -left[unit],
            )
            units += inner[:max(0, fill - len(units))]
            for unit in units:
                left[unit] -= 1
            rounds.append(units)
        return rounds

    def outer(*fields):
        return [(i, f) for f in fields for i in (3, 0)]

    def all_of(*fields):
        return [(i, f) for f in fields for i in (3, 0, 1, 2)]

    plan = [
        stretch(1, all_of(0), {}, 4)
        + stretch(1, outer(0, 1), {}, 7)
        + stretch(1, outer(0, 1, 2), {}, 7)
        + stretch(13, outer(0, 1), {(3, 2): 12, (3, 3): 13, (0, 2): 7, (0, 3): 7}, 7),
        stretch(1, outer(1, 2, 3), {}, 7),
        stretch(2, outer(2, 3), {}, 7),
        stretch(6, [(0, 2), (0, 3)], {}, 9),
        [],
    ]
    while any(left.values()):
        plan[-1] += stretch(1, [], {}, 8)
    return plan


def split(values):
    high = values.astype(jnp.bfloat16)
    low = (values - high.astype(jnp.float32)).astype(jnp.bfloat16)
    return high, low


def kernel(
    fields, mixing, classes,
    cells, east_halo, west_halo, north_halo, south_halo,
    limits, matrices, weights, steps, north_send, south_send,
    cell_sem, mix_sem, class_sem, send_sem, recv_sem,
):
    field_count, lons, lats, levels = fields.shape
    ops = mixing.shape[1]
    lon, lat = lax.axis_index("lon"), lax.axis_index("lat")
    lon_count, lat_count = lax.axis_size("lon"), lax.axis_size("lat")
    east = (lax.rem(lon + 1, lon_count), lat)
    west = (lax.rem(lon + lon_count - 1, lon_count), lat)
    north = (lon, lax.rem(lat + 1, lat_count))
    south = (lon, lax.rem(lat + lat_count - 1, lat_count))

    loads = []
    for f in range(field_count):
        loads += [
            pltpu.make_async_copy(mixing.at[f], matrices.at[f], mix_sem.at[f]),
            pltpu.make_async_copy(fields.at[f], cells.at[f], cell_sem.at[f]),
        ]
    loads.append(pltpu.make_async_copy(classes, steps, class_sem))
    for copy in loads:
        copy.start()

    barrier = pltpu.get_barrier_semaphore()
    for neighbour in (east, west, north, south):
        pl.semaphore_signal(barrier, inc=1, device_id=neighbour, device_id_type=MESH)

    for copy in loads:
        copy.wait()
    for i in range(lons):
        limits[i, pl.ds(0, lats), :] = jnp.broadcast_to(steps[pl.ds(i, 1), :] + 1, (levels, lats)).T
    limits[0, pl.ds(lats, PAD), :] = jnp.concatenate(
        [limits[i, pl.ds(row, 1), :] for row in (0, lats - 1) for i in (1, 2)]
        + [jnp.zeros((PAD - 4, levels), jnp.int32)],
        axis=0,
    )

    sends = []

    def send(source, target, device):
        slot = len(sends)
        copy = pltpu.make_async_remote_copy(
            src_ref=source, dst_ref=target, send_sem=send_sem.at[slot], recv_sem=recv_sem.at[slot],
            device_id=device, device_id_type=MESH,
        )
        sends.append(copy)
        return copy

    current, done = {}, {}

    def begin(f):
        for o in range(ops):
            pieces = jnp.concatenate(split(matrices[f, o]), axis=0).T
            weights[f, o, pl.ds(0, levels), :] = pieces
            weights[f, o, pl.ds(levels, levels), :] = pieces
        for i in range(lons):
            value = cells[f, i]
            if i == 0:
                value = jnp.concatenate(
                    [value]
                    + [cells[f, k, pl.ds(row, 1), :] for row in (0, lats - 1) for k in (1, 2)]
                    + [jnp.zeros((PAD - 4, levels), jnp.float32)],
                    axis=0,
                )
            current[i, f] = 0.5 * value
            done[i, f] = 0

    def finish(unit):
        i, f = unit
        value = current.pop(unit)
        cells[f, i] = value[:lats]
        if i == 0:
            for k in (1, 2):
                south_send[pl.ds(f * lons + k, 1), :] = value[lats + k - 1:lats + k]
                north_send[pl.ds(f * lons + k, 1), :] = value[lats + k + 1:lats + k + 2]
        if i in (0, 3):
            south_send[pl.ds(f * lons + i, 1), :] = value[:1]
            north_send[pl.ds(f * lons + i, 1), :] = value[lats - 1:lats]

    def step(units):
        pairs = {}
        for unit in units:
            pairs.setdefault((unit[0] in (1, 2), unit[1]), []).append(unit)
        values = {key: jnp.concatenate([current[unit] for unit in pair], axis=0) for key, pair in pairs.items()}
        for o in range(ops):
            for key in pairs:
                pieces = jnp.concatenate(split(values[key]), axis=1)
                mixed = jnp.dot(pieces, weights[key[1], o], preferred_element_type=jnp.float32)
                values[key] = jnp.tanh(mixed[:, :levels] + mixed[:, levels:])
        for key, pair in pairs.items():
            row = 0
            for unit in pair:
                height = current[unit].shape[0]
                active = limits[unit[0], pl.ds(0, height), :] > done[unit]
                current[unit] = jnp.where(active, values[key][row:row + height], current[unit])
                row += height
                done[unit] += 1

    edges, sent = [], {0: 0, 3: 0}
    for stretch in stretches(field_count):
        for units in stretch:
            for unit in units:
                if unit not in done:
                    begin(unit[1])
            step(units)
        over = [unit for unit in current if done[unit] == STEPS]
        for unit in over:
            finish(unit)
        if over and not sends:
            pl.semaphore_wait(barrier, 4)
        for i, halo, device in ((3, west_halo, east), (0, east_halo, west)):
            found = sorted(f for k, f in over if k == i)
            if found:
                chosen = pl.ds(found[0], len(found))
                send(cells.at[chosen, i], halo.at[chosen], device).start()
                sent[i] += len(found)
        if sent == {0: field_count, 3: field_count} and not edges:
            edges += [send(north_send, south_halo, north), send(south_send, north_halo, south)]

            @pl.when(lat < lat_count - 1)
            def _():
                edges[0].start()

            @pl.when(lat > 0)
            def _():
                edges[1].start()

    for copy in sends[:-2]:
        copy.wait()

    @pl.when(lat < lat_count - 1)
    def _():
        edges[0].wait_send()
        edges[1].wait_recv()

    @pl.when(lat > 0)
    def _():
        edges[1].wait_send()
        edges[0].wait_recv()


def smooth(cells, east_halo, west_halo, north_halo, south_halo, out, result, out_sem):
    field_count, lons, lats, levels = out.shape
    lat, lat_count = lax.axis_index("lat"), lax.axis_size("lat")
    row = lax.broadcasted_iota(jnp.int32, (lats, levels), 0)
    stores = []
    for f in range(field_count):
        field = [cells[f, i] for i in range(lons)]
        around = [west_halo[f]] + field + [east_halo[f]]
        for i in range(lons):
            cell = field[i]
            k = f * lons + i
            above = jnp.where(lat == lat_count - 1, cell[lats - 1:], north_halo[pl.ds(k, 1), :])
            below = jnp.where(lat == 0, cell[:1], south_halo[pl.ds(k, 1), :])
            northern = jnp.where(row == lats - 1, above, pltpu.roll(cell, lats - 1, 0))
            southern = jnp.where(row == 0, below, pltpu.roll(cell, 1, 0))
            result[f, i] = 0.4 * (cell + around[i] + around[i + 2] + northern + southern)
            copy = pltpu.make_async_copy(result.at[f, i], out.at[f, i], out_sem.at[k])
            copy.start()
            stores.append(copy)
    for copy in stores:
        copy.wait()


def per_device(fields, mixing, classes):
    field_count, lons, lats, levels = fields.shape
    ops = mixing.shape[1]
    f32, i32 = jnp.float32, jnp.int32
    halo = pltpu.VMEM((field_count, lats, levels), f32)
    edge = pltpu.VMEM((field_count * lons, levels), f32)
    copies = 2 + 2 * field_count
    rows = STEPS * ops * field_count * (lons * lats + PAD)
    in_hbm = pl.BlockSpec(memory_space=pltpu.HBM)
    in_vmem = pl.BlockSpec(memory_space=pltpu.VMEM)
    state = pl.pallas_call(
        kernel,
        out_shape=[pltpu.VMEM(fields.shape, f32), halo, halo, edge, edge],
        in_specs=[in_hbm] * 3,
        out_specs=[in_vmem] * 5,
        scratch_shapes=[
            pltpu.VMEM((lons, lats + PAD, levels), i32),
            pltpu.VMEM(mixing.shape, f32),
            pltpu.VMEM((field_count, ops, 2 * levels, 2 * levels), jnp.bfloat16),
            pltpu.VMEM((lons, lats), i32),
            edge, edge,
            pltpu.SemaphoreType.DMA((field_count,)),
            pltpu.SemaphoreType.DMA((field_count,)),
            pltpu.SemaphoreType.DMA,
            pltpu.SemaphoreType.DMA((copies,)),
            pltpu.SemaphoreType.DMA((copies,)),
        ],
        compiler_params=pltpu.CompilerParams(
            collective_id=0, has_side_effects=True, vmem_limit_bytes=32 * 2**20
        ),
        cost_estimate=pl.CostEstimate(
            flops=2 * rows * (2 * levels) ** 2, bytes_accessed=2 * 4 * fields.size, transcendentals=rows * levels
        ),
    )(*[pltpu.with_memory_space_constraint(x, pltpu.HBM) for x in (fields, mixing, classes)])
    return pl.pallas_call(
        smooth,
        out_shape=pltpu.HBM(fields.shape, f32),
        in_specs=[in_vmem] * 5,
        out_specs=in_hbm,
        scratch_shapes=[
            pltpu.VMEM(fields.shape, f32),
            pltpu.SemaphoreType.DMA((field_count * lons,)),
        ],
        compiler_params=pltpu.CompilerParams(vmem_limit_bytes=16 * 2**20),
        cost_estimate=pl.CostEstimate(flops=7 * fields.size, bytes_accessed=12 * fields.size, transcendentals=0),
    )(*state)


def solution(mesh):
    in_specs = (P(None, "lon", "lat", None), P(), P("lon", "lat"))
    out_specs = P(None, "lon", "lat", None)
    return jax.shard_map(
        per_device, mesh=mesh, in_specs=in_specs, out_specs=out_specs, check_vma=False
    )
```

```python
import functools

import jax
import jax.numpy as jnp
from jax import lax
from jax.experimental import pallas as pl
from jax.experimental.pallas import tpu as pltpu
from jax.sharding import PartitionSpec as P

STEPS = 16
PAD = 16
MESH = pl.DeviceIdType.MESH


def stretches(field_count):
    left = {(i, f): STEPS for f in range(field_count) for i in (3, 0, 1, 2)}

    def stretch(count, always, shares, fill):
        shares, rounds = dict(shares), []
        for _ in range(count):
            units = [unit for unit in always if left[unit]]
            some = sorted((unit for unit in shares if shares[unit]), key=lambda unit: -shares[unit])
            units += some[:max(0, fill - len(units))]
            for unit in units:
                if unit in shares:
                    shares[unit] -= 1
            inner = sorted(
                (unit for unit in left if unit[0] in (1, 2) and left[unit] and unit not in units),
                key=lambda unit: -left[unit],
            )
            units += inner[:max(0, fill - len(units))]
            for unit in units:
                left[unit] -= 1
            rounds.append(units)
        return rounds

    def outer(*fields):
        return [(i, f) for f in fields for i in (3, 0)]

    def all_of(*fields):
        return [(i, f) for f in fields for i in (3, 0, 1, 2)]

    plan = [
        stretch(1, all_of(0), {}, 4)
        + stretch(1, outer(0, 1), {}, 7)
        + stretch(1, outer(0, 1, 2), {}, 7)
        + stretch(13, outer(0, 1), {(3, 2): 12, (3, 3): 13, (0, 2): 7, (0, 3): 7}, 7),
        stretch(1, outer(1, 2, 3), {}, 7),
        stretch(2, outer(2, 3), {}, 7),
        stretch(6, [(0, 2), (0, 3)], {}, 9),
        [],
    ]
    while any(left.values()):
        plan[-1] += stretch(1, [], {}, 8)
    return plan


def split(values):
    high = values.astype(jnp.bfloat16)
    low = (values - high.astype(jnp.float32)).astype(jnp.bfloat16)
    return high, low


def kernel(
    fields, mixing, classes,
    partial, east_halo, west_halo, north_halo, south_halo,
    cells, limits, matrices, weights, steps, north_send, south_send,
    cell_sem, mix_sem, class_sem, send_sem, recv_sem,
):
    field_count, lons, lats, levels = fields.shape
    ops = mixing.shape[1]
    lon, lat = lax.axis_index("lon"), lax.axis_index("lat")
    lon_count, lat_count = lax.axis_size("lon"), lax.axis_size("lat")
    east = (lax.rem(lon + 1, lon_count), lat)
    west = (lax.rem(lon + lon_count - 1, lon_count), lat)
    north = (lon, lax.rem(lat + 1, lat_count))
    south = (lon, lax.rem(lat + lat_count - 1, lat_count))

    loads = []
    for f in range(field_count):
        loads += [
            pltpu.make_async_copy(mixing.at[f], matrices.at[f], mix_sem.at[f]),
            pltpu.make_async_copy(fields.at[f], cells.at[f], cell_sem.at[f]),
        ]
    loads.append(pltpu.make_async_copy(classes, steps, class_sem))
    for copy in loads:
        copy.start()

    barrier = pltpu.get_barrier_semaphore()
    for neighbour in (east, west, north, south):
        pl.semaphore_signal(barrier, inc=1, device_id=neighbour, device_id_type=MESH)

    for copy in loads:
        copy.wait()
    for i in range(lons):
        limits[i, pl.ds(0, lats), :] = jnp.broadcast_to(steps[pl.ds(i, 1), :] + 1, (levels, lats)).T
    limits[0, pl.ds(lats, PAD), :] = jnp.concatenate(
        [limits[i, pl.ds(row, 1), :] for row in (0, lats - 1) for i in (1, 2)]
        + [jnp.zeros((PAD - 4, levels), jnp.int32)],
        axis=0,
    )

    sends = []

    def send(source, target, device):
        slot = len(sends)
        copy = pltpu.make_async_remote_copy(
            src_ref=source, dst_ref=target, send_sem=send_sem.at[slot], recv_sem=recv_sem.at[slot],
            device_id=device, device_id_type=MESH,
        )
        sends.append(copy)
        return copy

    current, done = {}, {}

    def begin(f):
        for o in range(ops):
            pieces = jnp.concatenate(split(matrices[f, o]), axis=0).T
            weights[f, o, pl.ds(0, levels), :] = pieces
            weights[f, o, pl.ds(levels, levels), :] = pieces
        for i in range(lons):
            value = cells[f, i]
            if i == 0:
                value = jnp.concatenate(
                    [value]
                    + [cells[f, k, pl.ds(row, 1), :] for row in (0, lats - 1) for k in (1, 2)]
                    + [jnp.zeros((PAD - 4, levels), jnp.float32)],
                    axis=0,
                )
            current[i, f] = 0.5 * value
            done[i, f] = 0

    def finish(unit):
        i, f = unit
        value = current.pop(unit)
        cells[f, i] = value[:lats]
        if i == 0:
            for k in (1, 2):
                south_send[pl.ds(f * lons + k, 1), :] = value[lats + k - 1:lats + k]
                north_send[pl.ds(f * lons + k, 1), :] = value[lats + k + 1:lats + k + 2]
        if i in (0, 3):
            south_send[pl.ds(f * lons + i, 1), :] = value[:1]
            north_send[pl.ds(f * lons + i, 1), :] = value[lats - 1:lats]

    def step(units):
        pairs = {}
        for unit in units:
            pairs.setdefault((unit[0] in (1, 2), unit[1]), []).append(unit)
        values = {key: jnp.concatenate([current[unit] for unit in pair], axis=0) for key, pair in pairs.items()}
        for o in range(ops):
            for key in pairs:
                pieces = jnp.concatenate(split(values[key]), axis=1)
                mixed = jnp.dot(pieces, weights[key[1], o], preferred_element_type=jnp.float32)
                values[key] = jnp.tanh(mixed[:, :levels] + mixed[:, levels:])
        for key, pair in pairs.items():
            row = 0
            for unit in pair:
                height = current[unit].shape[0]
                active = limits[unit[0], pl.ds(0, height), :] > done[unit]
                current[unit] = jnp.where(active, values[key][row:row + height], current[unit])
                row += height
                done[unit] += 1

    edges, sent = [], {0: 0, 3: 0}
    for stretch in stretches(field_count):
        for units in stretch:
            for unit in units:
                if unit not in done:
                    begin(unit[1])
            step(units)
        over = [unit for unit in current if done[unit] == STEPS]
        for unit in over:
            finish(unit)
        if over and not sends:
            pl.semaphore_wait(barrier, 4)
        for i, halo, device in ((3, west_halo, east), (0, east_halo, west)):
            found = sorted(f for k, f in over if k == i)
            if found:
                chosen = pl.ds(found[0], len(found))
                send(cells.at[chosen, i], halo.at[chosen], device).start()
                sent[i] += len(found)
        if sent == {0: field_count, 3: field_count} and not edges:
            edges += [send(north_send, south_halo, north), send(south_send, north_halo, south)]

            @pl.when(lat < lat_count - 1)
            def _():
                edges[0].start()

            @pl.when(lat > 0)
            def _():
                edges[1].start()

    row = lax.broadcasted_iota(jnp.int32, (lats, levels), 0)
    for f in range(field_count):
        field = [cells[f, i] for i in range(lons)]
        for i in range(lons):
            northern = jnp.where(row == lats - 1, 0.0, pltpu.roll(field[i], lats - 1, 0))
            southern = jnp.where(row == 0, 0.0, pltpu.roll(field[i], 1, 0))
            total = field[i] + northern + southern
            for k in (i - 1, i + 1):
                if 0 <= k < lons:
                    total = total + field[k]
            partial[f, i] = 0.4 * total

    @pl.when(lat == lat_count - 1)
    def _():
        north_halo[...] = north_send[...]

    @pl.when(lat == 0)
    def _():
        south_halo[...] = south_send[...]

    for copy in sends[:-2]:
        copy.wait()

    @pl.when(lat < lat_count - 1)
    def _():
        edges[0].wait_send()
        edges[1].wait_recv()

    @pl.when(lat > 0)
    def _():
        edges[1].wait_send()
        edges[0].wait_recv()


def smooth(partial, east_halo, west_halo, north_halo, south_halo, out, result, out_sem):
    field_count, lons, lats, levels = out.shape
    stores = []
    for f in range(field_count):
        for i in range(lons):
            k = f * lons + i
            total = partial[f, i]
            if i == 0:
                total = total + 0.4 * west_halo[f]
            if i == lons - 1:
                total = total + 0.4 * east_halo[f]
            result[f, i] = total
            result[f, i, pl.ds(0, 1), :] = total[:1] + 0.4 * south_halo[pl.ds(k, 1), :]
            result[f, i, pl.ds(lats - 1, 1), :] = total[lats - 1:] + 0.4 * north_halo[pl.ds(k, 1), :]
            copy = pltpu.make_async_copy(result.at[f, i], out.at[f, i], out_sem.at[k])
            copy.start()
            stores.append(copy)
    for copy in stores:
        copy.wait()


def per_device(fields, mixing, classes):
    field_count, lons, lats, levels = fields.shape
    ops = mixing.shape[1]
    f32, i32 = jnp.float32, jnp.int32
    halo = pltpu.VMEM((field_count, lats, levels), f32)
    edge = pltpu.VMEM((field_count * lons, levels), f32)
    copies = 2 + 2 * field_count
    rows = STEPS * ops * field_count * (lons * lats + PAD)
    in_hbm = pl.BlockSpec(memory_space=pltpu.HBM)
    in_vmem = pl.BlockSpec(memory_space=pltpu.VMEM)
    state = pl.pallas_call(
        kernel,
        out_shape=[pltpu.VMEM(fields.shape, f32), halo, halo, edge, edge],
        in_specs=[in_hbm] * 3,
        out_specs=[in_vmem] * 5,
        scratch_shapes=[
            pltpu.VMEM(fields.shape, f32),
            pltpu.VMEM((lons, lats + PAD, levels), i32),
            pltpu.VMEM(mixing.shape, f32),
            pltpu.VMEM((field_count, ops, 2 * levels, 2 * levels), jnp.bfloat16),
            pltpu.VMEM((lons, lats), i32),
            edge, edge,
            pltpu.SemaphoreType.DMA((field_count,)),
            pltpu.SemaphoreType.DMA((field_count,)),
            pltpu.SemaphoreType.DMA,
            pltpu.SemaphoreType.DMA((copies,)),
            pltpu.SemaphoreType.DMA((copies,)),
        ],
        compiler_params=pltpu.CompilerParams(
            collective_id=0, has_side_effects=True, vmem_limit_bytes=32 * 2**20
        ),
        cost_estimate=pl.CostEstimate(
            flops=2 * rows * (2 * levels) ** 2, bytes_accessed=2 * 4 * fields.size, transcendentals=rows * levels
        ),
    )(*[pltpu.with_memory_space_constraint(x, pltpu.HBM) for x in (fields, mixing, classes)])
    return pl.pallas_call(
        smooth,
        out_shape=pltpu.HBM(fields.shape, f32),
        in_specs=[in_vmem] * 5,
        out_specs=in_hbm,
        scratch_shapes=[
            pltpu.VMEM(fields.shape, f32),
            pltpu.SemaphoreType.DMA((field_count * lons,)),
        ],
        compiler_params=pltpu.CompilerParams(vmem_limit_bytes=16 * 2**20),
        cost_estimate=pl.CostEstimate(flops=7 * fields.size, bytes_accessed=12 * fields.size, transcendentals=0),
    )(*state)


def solution(mesh):
    in_specs = (P(None, "lon", "lat", None), P(), P("lon", "lat"))
    out_specs = P(None, "lon", "lat", None)
    return jax.shard_map(
        per_device, mesh=mesh, in_specs=in_specs, out_specs=out_specs, check_vma=False
    )
```
